512 devices in a mesh: alpha: 32 (over y, x, core), beta: 16 (over z).
Axes of the slice: x: 4, y: 4, z: 16, core: 2. Of those that a mesh axis runs over, the one named last changes fastest.
Arguments:
- coeffs: bfloat16 [8192, 8192], P('alpha', 'beta'), may hold values from -6 to 6, as said below
- requests: int32 [32, 32, 16], P('alpha'), may hold values from 0 to 255, as said below
- repl_slot: int32 [32, 8192], P(None, 'alpha'), may hold values from 0 to 511, as said below
- repl_sign: int32 [32, 8192], P(None, 'alpha'), may hold values from -1 to 1
- pair_integrals: bfloat16 [32, 32], replicated, may hold values from -0.375 to 0.375
Outputs:
- sigma: float32 [8192, 8192], P('alpha', 'beta')
The draws below stay inside these ranges and needn't reach their ends.
Inputs may be any that keep to these rules, and one draw needn't show every extreme that they name: coeffs equals its transpose. Each list of requests names distinct strings first and is padded with 0 after them; every list holds at least one string. repl_slot always names a filled entry of its string's own tile's lists.
All inputs are finite; a program needn't handle non-finite values.
Results may differ from the reference program's by a relative error of at most 0.0029.
Values may be sent and summed in bfloat16 or wider, within the bound.
No kernel may reach another device: no remote copies, remote signals or barrier semaphores. Data moves between devices by JAX's collectives and lax.ppermute only.
A program may use at most 128 MiB of HBM per device.

```python
import jax
import jax.numpy as jnp
from jax import lax

A_DEV = 256
CAP = 16
P_SIZE = 32
NSTR = 8192


def request_counts(key):
    key = jax.random.fold_in(key, 11)
    first_key, second_key = jax.random.split(key)
    peers = NSTR // A_DEV
    lowest = max(1, CAP // 4)
    counts = jax.random.randint(first_key, (peers, peers), lowest, CAP + 1)
    offset = jax.random.randint(second_key, (), 0, peers)
    target = jnp.arange(peers)[:, None]
    source = jnp.arange(peers)[None, :]
    counts = jnp.where(source == (target + offset) % peers, CAP, counts)
    counts = jnp.where((target == 0) & (source == (offset + 1) % peers), 1, counts)
    return (counts, offset)


def draw_coeffs(key, part):
    key = jax.random.fold_in(key, 7)
    drawn = jnp.clip(jax.random.normal(key, (NSTR, NSTR), jnp.float32), -4.0, 4.0)
    return ((drawn + drawn.T) * 0.7071).astype(jnp.bfloat16)


def draw_requests(key, part):
    counts, offset = request_counts(key)
    key = jax.random.fold_in(key, 3)
    peers = NSTR // A_DEV
    raw = jax.random.randint(key, (peers, peers, A_DEV), 0, 1 << 20)
    position = jnp.arange(A_DEV)[None, None, :]
    scores = raw * A_DEV + position
    target = jnp.arange(peers)[:, None, None]
    source = jnp.arange(peers)[None, :, None]
    first = (target == 0) & (source == offset % peers) & (position == A_DEV - 1)
    scores = jnp.where(first, -1, scores)
    order = jnp.argsort(scores, axis=-1, stable=True)[:, :, :CAP].astype(jnp.int32)
    live = jnp.arange(CAP)[None, None, :] < counts[:, :, None]
    return jnp.where(live, order, 0).astype(jnp.int32)


def draw_repl_slot(key, part):
    counts, offset = request_counts(key)
    key = jax.random.fold_in(key, 5)
    first_key, second_key = jax.random.split(key)
    peers = NSTR // A_DEV
    target = jnp.broadcast_to((jnp.arange(NSTR) // A_DEV)[None, :], (P_SIZE, NSTR))
    source = jax.random.randint(first_key, (P_SIZE, NSTR), 0, peers)
    have = counts[target, source]
    column = jax.random.randint(second_key, (P_SIZE, NSTR), 0, 1 << 20) % have
    slot = source * CAP + column
    top_target = (peers - 1 - offset) % peers
    slot = slot.at[0, top_target * A_DEV].set(peers * CAP - 1)
    slot = slot.at[1, 0].set(0)
    return slot.astype(jnp.int32)


def set_ends(result, stream_key, smallest, high):
    longest = result.shape.index(max(result.shape))
    spots = []
    for shift in (0, 1):
        where = [jax.random.randint(jax.random.fold_in(stream_key, axis), (), 0, length) for axis, length in enumerate(result.shape)]
        where[longest] = (where[longest] + shift) % result.shape[longest]
        spots.append(tuple(where))
    return result.at[spots[0]].set(smallest).at[spots[1]].set(high)


def normal_values(rng, shape, spread, limit, kind=jnp.bfloat16):
    values = jax.random.normal(rng, shape, jnp.float32) * spread
    return jnp.minimum(jnp.maximum(values, -limit), limit).astype(kind)


def setup_inputs(seed: int = 0) -> dict:
    keys = jax.random.split(jax.random.key(seed), 6)
    return {
        "coeffs": draw_coeffs(jax.random.fold_in(keys[5], 71), 0),
        "requests": draw_requests(jax.random.fold_in(keys[5], 71), 0),
        "repl_slot": draw_repl_slot(jax.random.fold_in(keys[5], 71), 0),
        "repl_sign": set_ends(jax.random.randint(keys[3], (P_SIZE, NSTR), -1, 2), jax.random.fold_in(keys[3], 1), -1, 1).astype(jnp.int32),
        "pair_integrals": normal_values(keys[4], (P_SIZE, P_SIZE), (8 * P_SIZE) ** -0.5, 0.375),
    }


def reference(coeffs, requests, repl_slot, repl_sign, pair_integrals):
    count = coeffs.shape[0]
    tiles = count // A_DEV
    source = repl_slot // CAP
    column = repl_slot % CAP
    target = jnp.broadcast_to((jnp.arange(count, dtype=jnp.int32) // A_DEV)[None, :], repl_slot.shape).astype(jnp.int32)
    src = (source * A_DEV + requests[target, source, column]).astype(jnp.int32)
    gains = pair_integrals.astype(jnp.float32)
    signs = repl_sign.astype(jnp.float32)

    def step(total, block):
        start = (block * A_DEV).astype(jnp.int32)
        src_block = lax.dynamic_slice_in_dim(src, start, A_DEV, 1)
        sign_block = lax.dynamic_slice_in_dim(signs, start, A_DEV, 1)
        moved = sign_block[:, :, None] * coeffs[src_block].astype(jnp.float32)
        mixed = jnp.einsum("qp,pan->qan", gains, moved, precision=lax.Precision.HIGHEST)
        mixed = mixed.astype(jnp.bfloat16).astype(jnp.float32)
        total = total.at[src_block].add(sign_block[:, :, None] * mixed)
        return total, None

    half_sigma, _ = lax.scan(step, jnp.zeros((count, count), jnp.float32), jnp.arange(tiles, dtype=jnp.int32))
    return half_sigma + half_sigma.T
```

```python
import jax
import jax.numpy as jnp
from jax import lax
from jax.experimental import pallas as pl
from jax.experimental.pallas import tpu as pltpu
from jax.sharding import PartitionSpec as P

F32 = jnp.float32
BF16 = jnp.bfloat16
VMEM = pltpu.VMEM


def flat_row(table, columns):
    n, m = table.shape
    width = n * m
    lane = lax.broadcasted_iota(jnp.int32, (m, width), 1)
    pick = (lane % m == lax.broadcasted_iota(jnp.int32, (m, width), 0)).astype(BF16)
    wide = jnp.dot(table.astype(F32).astype(BF16), pick, preferred_element_type=F32)
    lane = lax.broadcasted_iota(jnp.int32, (n, width), 1)
    mine = lane // m == lax.broadcasted_iota(jnp.int32, (n, width), 0)
    return jnp.sum(jnp.where(mine, wide, 0.0), axis=0, keepdims=True)


def one_hot(row, count):
    width = row.shape[1]
    lines = lax.broadcasted_iota(jnp.int32, (count, width), 0).astype(F32)
    return (lines == row).astype(F32).astype(BF16)


def coupling_kernel(slot_ref, sign_ref, kron_ref, high_ref, low_ref, total_ref):
    chunks, lanes = slot_ref.shape
    width = total_ref.shape[0]
    side = kron_ref.shape[0]
    line = lax.broadcasted_iota(jnp.int32, (16, lanes), 0).astype(F32).astype(BF16)
    total_ref[...] = jnp.zeros_like(total_ref)

    def step(c, carry):
        slots = (slot_ref[pl.ds(c, 1), :] - width // 2).astype(F32)
        signs = sign_ref[pl.ds(c, 1), :].astype(F32)
        slots = jnp.broadcast_to(slots, (16, lanes)).astype(BF16)
        signs = jnp.broadcast_to(signs, (16, lanes)).astype(BF16)
        zero = jnp.zeros((16, lanes), BF16)
        rows = []
        for k in range(width // 16):
            base = jnp.asarray(16 * k - width // 2, BF16)
            rows.append(jnp.where(slots == line + base, signs, zero))
        table = jnp.concatenate(rows, axis=0)
        mixed = [
            jnp.dot(table[:, n : n + side], kron_ref[...], preferred_element_type=F32).astype(BF16)
            for n in range(0, lanes, side)
        ]
        mixed = jnp.concatenate(mixed, axis=1)
        total_ref[...] += lax.dot_general(
            table, mixed, (((1,), (1,)), ((), ())), preferred_element_type=F32
        )
        return carry

    lax.fori_loop(0, chunks, step, 0)
    high = total_ref[...].astype(BF16)
    high_ref[...] = high
    low_ref[...] = (total_ref[...] - high.astype(F32)).astype(BF16)


def gather_kernel(asked_ref, coeffs_ref, found_ref):
    rows = coeffs_ref.shape[0]
    table = one_hot(flat_row(asked_ref[...], rows), rows)
    found = lax.dot_general(
        table, coeffs_ref[...], (((0,), (0,)), ((), ())), preferred_element_type=F32
    )
    found_ref[...] = found.astype(BF16)


def contributions_kernel(plane_ref, high_ref, low_ref, fetched_ref, extra_ref, own_ref):
    sites, two_cap, half = extra_ref.shape
    chips = sites // 2
    fetched = fetched_ref[...]
    contrib = jnp.dot(high_ref[...], fetched, preferred_element_type=F32)
    contrib += jnp.dot(low_ref[...], fetched, preferred_element_type=F32)
    own_ref[...] = contrib.astype(BF16)
    plane = plane_ref[0]
    for j in range(chips):
        for h in range(2):
            chip = lax.rem(j + 2 * chips - plane - h * (chips // 2), chips)
            start = pl.multiple_of(chip * two_cap, two_cap)
            extra_ref[2 * j + h] = own_ref[pl.ds(start, two_cap), h * half : (h + 1) * half]


def turned_kernel(cap, asked_ref, extra_ref, turned_ref):
    rows, cols = turned_ref.shape
    asked = flat_row(asked_ref[...], rows)
    width = asked.shape[1]
    lane = lax.broadcasted_iota(jnp.int32, (1, width), 1)
    core = (lane // cap) % 2
    table = one_hot(asked + (core * rows).astype(F32), cols)
    summed = jnp.dot(table, extra_ref[...], preferred_element_type=F32)
    turned_ref[...] = summed.T.astype(BF16)


def own_kernel(asked_ref, returned_ref, half_ref):
    rows = half_ref.shape[0]
    table = one_hot(flat_row(asked_ref[...], rows), rows)
    half_ref[...] = jnp.dot(table, returned_ref[...], preferred_element_type=F32)


def call(kernel, outs, operands, flops, moved, scratch=(), scalars=0):
    in_specs = [pl.BlockSpec(memory_space=pltpu.SMEM)] * scalars
    in_specs += [pl.BlockSpec(memory_space=VMEM)] * (len(operands) - scalars)
    many = isinstance(outs, (list, tuple))
    return pl.pallas_call(
        kernel,
        out_shape=outs,
        in_specs=in_specs,
        out_specs=[pl.BlockSpec(memory_space=VMEM)] * len(outs) if many else pl.BlockSpec(memory_space=VMEM),
        scratch_shapes=list(scratch),
        compiler_params=pltpu.CompilerParams(vmem_limit_bytes=40 * 2**20),
        cost_estimate=pl.CostEstimate(flops=flops, bytes_accessed=moved, transcendentals=0),
    )(*operands)


def local(coeffs, requests, repl_slot, repl_sign, pair_integrals):
    rows, cols = coeffs.shape
    peers = lax.axis_size("alpha")
    chips = lax.axis_size("beta")
    plane = lax.axis_index("beta").astype(jnp.int32)
    wanted = requests[0]
    cap = wanted.shape[1]
    width = peers * cap
    pairs = repl_slot.shape[0]

    by_chip = wanted.reshape(chips, 2 * cap)
    twice = jnp.concatenate([by_chip, by_chip], axis=0)
    shifted = [
        lax.dynamic_slice_in_dim(twice, (2 * chips - plane - h * (chips // 2)) % chips, chips, 0)
        for h in range(2)
    ]
    shifted = jnp.stack(shifted, axis=1).reshape(peers, 2 * cap)
    asked = lax.all_to_all(
        jnp.concatenate([wanted, shifted], axis=1), "alpha", split_axis=0, concat_axis=0, tiled=True
    )
    asked_own, asked_site = asked[:, :cap], asked[:, cap:]

    lanes = 1024 if (rows * pairs) % 1024 == 0 else rows * pairs
    group = 256 // pairs
    slot_rows = repl_slot.T.reshape(-1, lanes)
    sign_rows = repl_sign.T.reshape(-1, lanes)
    kron = jnp.kron(jnp.eye(group, dtype=BF16), pair_integrals.T)
    square = jax.ShapeDtypeStruct((width, width), BF16)
    high, low = call(
        coupling_kernel,
        [square, square],
        (slot_rows, sign_rows, kron),
        2 * rows * pairs * width * (width + 256),
        4 * width * width,
        scratch=[VMEM((width, width), F32)],
    )

    found = call(
        gather_kernel,
        jax.ShapeDtypeStruct((width, cols), BF16),
        (asked_own, coeffs),
        2 * width * rows * cols,
        2 * (width + rows) * cols,
    )
    fetched = lax.all_to_all(
        found.reshape(peers, cap, cols), "alpha", split_axis=0, concat_axis=0, tiled=True
    ).reshape(width, cols)

    extra, own = call(
        contributions_kernel,
        [jax.ShapeDtypeStruct((peers, 2 * cap, cols // 2), BF16), jax.ShapeDtypeStruct((width, cols), BF16)],
        (plane.reshape(1), high, low, fetched),
        4 * width * width * cols,
        4 * width * width + 6 * width * cols,
        scalars=1,
    )
    extra = lax.all_to_all(extra, "alpha", split_axis=0, concat_axis=0, tiled=True)

    turned = call(
        lambda *refs: turned_kernel(cap, *refs),
        jax.ShapeDtypeStruct((rows, cols), BF16),
        (asked_site, extra.reshape(2 * width, cols // 2)),
        2 * cols * width * cols,
        2 * (width + rows) * cols,
    )
    own, turned = lax.optimization_barrier((own, turned))
    places = []
    for j in range(chips):
        for h in range(2):
            for z in range(chips):
                l = (j - z - h * (chips // 2)) % chips
                places.append(((2 * j + h) * chips + z, (2 * z + h) * chips + l))
    turned = lax.ppermute(turned, ("alpha", "beta"), places)
    returned = lax.all_to_all(
        own.reshape(peers, cap, cols), "alpha", split_axis=0, concat_axis=0, tiled=True
    ).reshape(width, cols)
    half_sigma = call(
        own_kernel,
        jax.ShapeDtypeStruct((rows, cols), F32),
        (asked_own, returned),
        2 * width * rows * cols,
        2 * width * cols + 4 * rows * cols,
    )
    return half_sigma + turned.astype(F32)


def solution(mesh):
    in_specs = (P("alpha", "beta"), P("alpha", None, None), P(None, "alpha"), P(None, "alpha"), P())
    out_specs = P("alpha", "beta")
    return jax.shard_map(local, mesh=mesh, in_specs=in_specs, out_specs=out_specs, check_vma=False)
```

```python
import jax
import jax.numpy as jnp
from jax import lax
from jax.experimental import pallas as pl
from jax.experimental.pallas import tpu as pltpu
from jax.sharding import PartitionSpec as P

F32 = jnp.float32
BF16 = jnp.bfloat16
VMEM = pltpu.VMEM


def flat_row(table, columns):
    n, m = table.shape
    width = n * m
    lane = lax.broadcasted_iota(jnp.int32, (m, width), 1)
    pick = (lane % m == lax.broadcasted_iota(jnp.int32, (m, width), 0)).astype(BF16)
    wide = jnp.dot(table.astype(F32).astype(BF16), pick, preferred_element_type=F32)
    lane = lax.broadcasted_iota(jnp.int32, (n, width), 1)
    mine = lane // m == lax.broadcasted_iota(jnp.int32, (n, width), 0)
    return jnp.sum(jnp.where(mine, wide, 0.0), axis=0, keepdims=True)


def one_hot(row, count):
    width = row.shape[1]
    lines = lax.broadcasted_iota(jnp.int32, (count, width), 0).astype(F32)
    return (lines == row).astype(F32).astype(BF16)


def ask_kernel(wanted_ref, ask_ref):
    cap, peers = wanted_ref.shape
    chips = peers // 2
    plane = lax.axis_index("beta")
    site = lax.broadcasted_iota(jnp.int32, (peers, peers), 0)
    tile = lax.broadcasted_iota(jnp.int32, (peers, peers), 1)
    chip = site // 2 - plane - (site % 2) * (chips // 2)
    chip = jnp.where(chip < 0, chip + chips, chip)
    chip = jnp.where(chip < 0, chip + chips, chip)
    wanted = wanted_ref[...].astype(F32).astype(BF16)
    for part, source in enumerate((site, 2 * chip, 2 * chip + 1)):
        pick = (tile == source).astype(F32).astype(BF16)
        lists = lax.dot_general(pick, wanted, (((1,), (1,)), ((), ())), preferred_element_type=F32)
        ask_ref[:, part * cap : (part + 1) * cap] = lists.astype(jnp.int32)


def coupling_kernel(slot_ref, sign_ref, kron_ref, high_ref, low_ref, total_ref):
    chunks, lanes = slot_ref.shape
    width = total_ref.shape[0]
    side = kron_ref.shape[0]
    line = lax.broadcasted_iota(jnp.int32, (16, lanes), 0).astype(F32).astype(BF16)
    total_ref[...] = jnp.zeros_like(total_ref)

    def step(c, carry):
        slots = (slot_ref[pl.ds(c, 1), :] - width // 2).astype(F32)
        signs = sign_ref[pl.ds(c, 1), :].astype(F32)
        slots = jnp.broadcast_to(slots, (16, lanes)).astype(BF16)
        signs = jnp.broadcast_to(signs, (16, lanes)).astype(BF16)
        zero = jnp.zeros((16, lanes), BF16)
        rows = []
        for k in range(width // 16):
            base = jnp.asarray(16 * k - width // 2, BF16)
            rows.append(jnp.where(slots == line + base, signs, zero))
        table = jnp.concatenate(rows, axis=0)
        mixed = [
            jnp.dot(table[:, n : n + side], kron_ref[...], preferred_element_type=F32).astype(BF16)
            for n in range(0, lanes, side)
        ]
        mixed = jnp.concatenate(mixed, axis=1)
        total_ref[...] += lax.dot_general(
            table, mixed, (((1,), (1,)), ((), ())), preferred_element_type=F32
        )
        return carry

    lax.fori_loop(0, chunks, step, 0)
    high = total_ref[...].astype(BF16)
    high_ref[...] = high
    low_ref[...] = (total_ref[...] - high.astype(F32)).astype(BF16)


def gather_kernel(asked_ref, coeffs_ref, found_ref):
    rows = coeffs_ref.shape[0]
    peers, cap = asked_ref.shape
    line = lax.broadcasted_iota(jnp.int32, (cap, cap), 0)
    same = (line == lax.broadcasted_iota(jnp.int32, (cap, cap), 1)).astype(F32).astype(BF16)
    asked = asked_ref[...].astype(F32).astype(BF16)
    asked = lax.dot_general(same, asked, (((1,), (1,)), ((), ())), preferred_element_type=F32)
    lane = lax.broadcasted_iota(jnp.int32, (cap, rows), 1).astype(F32)
    table = [(asked[:, t : t + 1] == lane).astype(F32).astype(BF16) for t in range(peers)]
    found = jnp.dot(jnp.concatenate(table, axis=0), coeffs_ref[...], preferred_element_type=F32)
    found_ref[...] = found.astype(BF16)


def contributions_kernel(high_ref, low_ref, fetched_ref, sites_ref, owners_ref):
    sites, two_cap, half = sites_ref.shape
    chips = sites // 2
    plane = lax.axis_index("beta")
    fetched = fetched_ref[...]
    contrib = jnp.dot(high_ref[...], fetched, preferred_element_type=F32)
    contrib += jnp.dot(low_ref[...], fetched, preferred_element_type=F32)
    owners_ref[...] = contrib.astype(BF16)
    for j in range(chips):
        for h in range(2):
            chip = lax.rem(j + 2 * chips - plane - h * (chips // 2), chips)
            start = pl.multiple_of(chip * two_cap, two_cap)
            sites_ref[2 * j + h] = owners_ref[pl.ds(start, two_cap), h * half : (h + 1) * half]


def site_kernel(cap, asked_ref, contrib_ref, sent_ref):
    cols, rows = sent_ref.shape
    asked = flat_row(asked_ref[...], rows)
    lane = lax.broadcasted_iota(jnp.int32, asked.shape, 1)
    core = (lane // cap) % 2
    table = one_hot(asked + (core * rows).astype(F32), cols)
    sent_ref[...] = jnp.dot(table, contrib_ref[...], preferred_element_type=F32).astype(BF16)


def turn_kernel(sent_ref, turned_ref):
    turned_ref[...] = sent_ref[...].astype(F32).T


def from_third(chips):
    source, place = lax.axis_index("alpha") // 2, lax.axis_index("beta")
    return jnp.logical_and(source < chips // 2, place < chips // 2)


def choose_kernel(first_ref, second_ref, turned_ref):
    chips = lax.axis_size("beta")
    from_first = lax.axis_index("alpha") // 2 < chips // 2

    @pl.when(from_first)
    def _():
        turned_ref[...] = first_ref[...]

    @pl.when(jnp.logical_not(from_first))
    def _():
        turned_ref[...] = second_ref[...].astype(F32).T


def own_kernel(asked_ref, contrib_ref, turned_ref, part_ref):
    rows = part_ref.shape[0]
    table = one_hot(flat_row(asked_ref[...], rows), rows)
    part_ref[...] = jnp.dot(table, contrib_ref[...], preferred_element_type=F32) + turned_ref[...]


def sigma_kernel(part_ref, third_ref, sigma_ref):
    third = from_third(lax.axis_size("beta"))

    @pl.when(third)
    def _():
        sigma_ref[...] = part_ref[...] + third_ref[...].astype(F32).T

    @pl.when(jnp.logical_not(third))
    def _():
        sigma_ref[...] = part_ref[...]


def call(kernel, outs, operands, flops, moved, scratch=()):
    many = isinstance(outs, (list, tuple))
    spec = pl.BlockSpec(memory_space=VMEM)
    return pl.pallas_call(
        kernel,
        out_shape=outs,
        in_specs=[spec] * len(operands),
        out_specs=[spec] * len(outs) if many else spec,
        scratch_shapes=list(scratch),
        compiler_params=pltpu.CompilerParams(vmem_limit_bytes=40 * 2**20),
        cost_estimate=pl.CostEstimate(flops=flops, bytes_accessed=moved, transcendentals=0),
    )(*operands)


def local(coeffs, requests, repl_slot, repl_sign, pair_integrals):
    rows, cols = coeffs.shape
    peers = lax.axis_size("alpha")
    chips = lax.axis_size("beta")
    wanted = requests[0]
    cap = wanted.shape[1]
    width = peers * cap
    pairs = repl_slot.shape[0]

    ask = call(
        ask_kernel,
        jax.ShapeDtypeStruct((peers, 3 * cap), jnp.int32),
        (wanted.T,),
        6 * peers * peers * cap,
        16 * peers * cap,
    )
    asked = lax.all_to_all(ask, "alpha", split_axis=0, concat_axis=0, tiled=True)
    asked_rows, asked_site = asked[:, :cap], asked[:, cap:]

    lanes = 1024 if (rows * pairs) % 1024 == 0 else rows * pairs
    group = 256 // pairs
    slot_rows = repl_slot.T.reshape(-1, lanes)
    sign_rows = repl_sign.T.reshape(-1, lanes)
    kron = jnp.kron(jnp.eye(group, dtype=BF16), pair_integrals.T)
    square = jax.ShapeDtypeStruct((width, width), BF16)
    high, low = call(
        coupling_kernel,
        [square, square],
        (slot_rows, sign_rows, kron),
        2 * rows * pairs * width * (width + 256),
        4 * width * width,
        scratch=[VMEM((width, width), F32)],
    )

    found = call(
        gather_kernel,
        jax.ShapeDtypeStruct((width, cols), BF16),
        (asked_rows, coeffs),
        2 * width * rows * cols,
        2 * (width + rows) * cols,
    )
    fetched = lax.all_to_all(
        found.reshape(peers, cap, cols), "alpha", split_axis=0, concat_axis=0, tiled=True
    ).reshape(width, cols)

    to_sites, to_owners = call(
        contributions_kernel,
        [jax.ShapeDtypeStruct((peers, 2 * cap, cols // 2), BF16), jax.ShapeDtypeStruct((width, cols), BF16)],
        (high, low, fetched),
        4 * width * width * cols,
        4 * width * width + 6 * width * cols,
    )

    def site_sums(to_sites):
        to_sites = lax.all_to_all(to_sites, "alpha", split_axis=0, concat_axis=0, tiled=True)
        return call(
            lambda *refs: site_kernel(cap, *refs),
            jax.ShapeDtypeStruct((cols, rows), BF16),
            (asked_site, to_sites.reshape(2 * width, cols // 2)),
            2 * cols * width * cols,
            2 * (width + rows) * cols,
        )

    def nothing(to_sites):
        return jnp.zeros((cols, rows), BF16)

    places = [], [], []
    for j in range(chips):
        for h in range(2):
            for z in range(chips):
                l = (j - z - h * (chips // 2)) % chips
                part = 1 if 2 * z >= chips else 0 if 2 * l >= chips else 2
                places[part].append(((2 * j + h) * chips + z, (2 * z + h) * chips + l))
    axes = ("alpha", "beta")
    is_first = lax.axis_index("beta") < chips // 2
    first = lax.cond(is_first, site_sums, nothing, to_sites)
    first, to_sites = lax.optimization_barrier((first, to_sites))
    second = lax.cond(is_first, nothing, site_sums, to_sites)
    to_owners, second = lax.optimization_barrier((to_owners, second))
    third = lax.ppermute(first, axes, places[2])
    first = lax.ppermute(first, axes, places[0])
    second = lax.ppermute(second, axes, places[1])
    to_owners = lax.all_to_all(
        to_owners.reshape(peers, cap, cols), "alpha", split_axis=0, concat_axis=0, tiled=True
    )
    block = jax.ShapeDtypeStruct((rows, cols), F32)
    first = call(turn_kernel, block, (first,), 15 * 10**8, 6 * rows * cols)
    turned = call(choose_kernel, block, (first, second), 32 * 10**8, 10 * rows * cols)
    part = call(
        own_kernel, block, (asked_rows, to_owners.reshape(width, cols), turned), 3 * 10**10, 10 * rows * cols
    )
    return call(sigma_kernel, block, (part, third), rows * cols, 10 * rows * cols)


def solution(mesh):
    in_specs = (P("alpha", "beta"), P("alpha", None, None), P(None, "alpha"), P(None, "alpha"), P())
    out_specs = P("alpha", "beta")
    return jax.shard_map(local, mesh=mesh, in_specs=in_specs, out_specs=out_specs, check_vma=False)
```

```python
import jax
import jax.numpy as jnp
from jax import lax
from jax.experimental import pallas as pl
from jax.experimental.pallas import tpu as pltpu
from jax.sharding import PartitionSpec as P

F32 = jnp.float32
BF16 = jnp.bfloat16
VMEM = pltpu.VMEM


def flat_row(table, columns):
    n, m = table.shape
    width = n * m
    lane = lax.broadcasted_iota(jnp.int32, (m, width), 1)
    pick = (lane % m == lax.broadcasted_iota(jnp.int32, (m, width), 0)).astype(BF16)
    wide = jnp.dot(table.astype(F32).astype(BF16), pick, preferred_element_type=F32)
    lane = lax.broadcasted_iota(jnp.int32, (n, width), 1)
    mine = lane // m == lax.broadcasted_iota(jnp.int32, (n, width), 0)
    return jnp.sum(jnp.where(mine, wide, 0.0), axis=0, keepdims=True)


def one_hot(row, count):
    width = row.shape[1]
    lines = lax.broadcasted_iota(jnp.int32, (count, width), 0).astype(F32)
    return (lines == row).astype(F32).astype(BF16)


def ask_kernel(from_ref, ask_ref, wanted_ref):
    pltpu.sync_copy(from_ref, wanted_ref)
    cap, peers = wanted_ref.shape
    chips = peers // 2
    plane = lax.axis_index("beta")
    site = lax.broadcasted_iota(jnp.int32, (peers, peers), 0)
    tile = lax.broadcasted_iota(jnp.int32, (peers, peers), 1)
    chip = site // 2 - plane - (site % 2) * (chips // 2)
    chip = jnp.where(chip < 0, chip + chips, chip)
    chip = jnp.where(chip < 0, chip + chips, chip)
    wanted = wanted_ref[...].astype(F32).astype(BF16)
    for part, source in enumerate((site, 2 * chip, 2 * chip + 1)):
        pick = (tile == source).astype(F32).astype(BF16)
        lists = lax.dot_general(pick, wanted, (((1,), (1,)), ((), ())), preferred_element_type=F32)
        ask_ref[:, part * cap : (part + 1) * cap] = lists.astype(jnp.int32)


def coupling_kernel(slot_ref, sign_ref, kron_ref, high_ref, low_ref, total_ref):
    chunks, lanes = slot_ref.shape
    width = total_ref.shape[0]
    side = kron_ref.shape[0]
    line = lax.broadcasted_iota(jnp.int32, (16, lanes), 0).astype(F32).astype(BF16)
    total_ref[...] = jnp.zeros_like(total_ref)

    def step(c, carry):
        slots = (slot_ref[pl.ds(c, 1), :] - width // 2).astype(F32)
        signs = sign_ref[pl.ds(c, 1), :].astype(F32)
        slots = jnp.broadcast_to(slots, (16, lanes)).astype(BF16)
        signs = jnp.broadcast_to(signs, (16, lanes)).astype(BF16)
        zero = jnp.zeros((16, lanes), BF16)
        rows = []
        for k in range(width // 16):
            base = jnp.asarray(16 * k - width // 2, BF16)
            rows.append(jnp.where(slots == line + base, signs, zero))
        table = jnp.concatenate(rows, axis=0)
        mixed = [
            jnp.dot(table[:, n : n + side], kron_ref[...], preferred_element_type=F32).astype(BF16)
            for n in range(0, lanes, side)
        ]
        mixed = jnp.concatenate(mixed, axis=1)
        total_ref[...] += lax.dot_general(
            table, mixed, (((1,), (1,)), ((), ())), preferred_element_type=F32
        )
        return carry

    lax.fori_loop(0, chunks, step, 0)
    high = total_ref[...].astype(BF16)
    high_ref[...] = high
    low_ref[...] = (total_ref[...] - high.astype(F32)).astype(BF16)


def gather_kernel(asked_ref, coeffs_ref, found_ref, held_ref, sems):
    rows = coeffs_ref.shape[0]
    peers, cap = asked_ref.shape
    pieces = sems.shape[0]
    line = lax.broadcasted_iota(jnp.int32, (cap, cap), 0)
    same = (line == lax.broadcasted_iota(jnp.int32, (cap, cap), 1)).astype(F32).astype(BF16)
    asked = asked_ref[...].astype(F32).astype(BF16)
    asked = lax.dot_general(same, asked, (((1,), (1,)), ((), ())), preferred_element_type=F32)
    lane = lax.broadcasted_iota(jnp.int32, (cap, rows), 1).astype(F32)
    step = peers // pieces
    copies = []
    for n in range(pieces):
        tiles = range(n * step, (n + 1) * step)
        table = [(asked[:, t : t + 1] == lane).astype(F32).astype(BF16) for t in tiles]
        found = jnp.dot(jnp.concatenate(table, axis=0), coeffs_ref[...], preferred_element_type=F32)
        piece = pl.ds(n * step * cap, step * cap)
        held_ref[piece, :] = found.astype(BF16)
        copies.append(pltpu.make_async_copy(held_ref.at[piece, :], found_ref.at[piece, :], sems.at[n]))
        copies[n].start()
    for copy in copies:
        copy.wait()


def contributions_kernel(high_ref, low_ref, fetched_ref, sites_ref, owners_ref):
    sites, two_cap, half = sites_ref.shape
    chips = sites // 2
    plane = lax.axis_index("beta")
    fetched = fetched_ref[...]
    contrib = jnp.dot(high_ref[...], fetched, preferred_element_type=F32)
    contrib += jnp.dot(low_ref[...], fetched, preferred_element_type=F32)
    owners_ref[...] = contrib.astype(BF16)
    for j in range(chips):
        for h in range(2):
            chip = lax.rem(j + 2 * chips - plane - h * (chips // 2), chips)
            start = pl.multiple_of(chip * two_cap, two_cap)
            sites_ref[2 * j + h] = owners_ref[pl.ds(start, two_cap), h * half : (h + 1) * half]


def site_kernel(cap, asked_ref, contrib_ref, sent_ref):
    cols, rows = sent_ref.shape
    asked = flat_row(asked_ref[...], rows)
    lane = lax.broadcasted_iota(jnp.int32, asked.shape, 1)
    core = (lane // cap) % 2
    table = one_hot(asked + (core * rows).astype(F32), cols)
    sent_ref[...] = jnp.dot(table, contrib_ref[...], preferred_element_type=F32).astype(BF16)


def copy_kernel(from_ref, to_ref):
    to_ref[...] = from_ref[...]


def turn_kernel(sent_ref, turned_ref):
    turned_ref[...] = sent_ref[...].astype(F32).T


def from_third(chips):
    source, place = lax.axis_index("alpha") // 2, lax.axis_index("beta")
    return jnp.logical_and(source < chips // 2, place < chips // 2)


def choose_kernel(first_ref, second_ref, turned_ref):
    chips = lax.axis_size("beta")
    from_first = lax.axis_index("alpha") // 2 < chips // 2

    @pl.when(from_first)
    def _():
        turned_ref[...] = first_ref[...]

    @pl.when(jnp.logical_not(from_first))
    def _():
        turned_ref[...] = second_ref[...].astype(F32).T


def own_kernel(asked_ref, contrib_ref, turned_ref, part_ref):
    rows = part_ref.shape[0]
    table = one_hot(flat_row(asked_ref[...], rows), rows)
    part_ref[...] = jnp.dot(table, contrib_ref[...], preferred_element_type=F32) + turned_ref[...]


def sigma_kernel(part_ref, third_ref, sigma_ref, held_ref):
    @pl.when(from_third(lax.axis_size("beta")))
    def _():
        pltpu.sync_copy(part_ref, held_ref)
        held_ref[...] += third_ref[...].astype(F32).T
        pltpu.sync_copy(held_ref, sigma_ref)


def call(kernel, outs, operands, flops, moved, scratch=(), spaces=(), aliases=None, out_space=VMEM):
    many = isinstance(outs, (list, tuple))
    spec = pl.BlockSpec(memory_space=out_space)
    spaces = tuple(spaces) + (VMEM,) * (len(operands) - len(spaces))
    return pl.pallas_call(
        kernel,
        out_shape=outs,
        in_specs=[pl.BlockSpec(memory_space=space) for space in spaces],
        out_specs=[spec] * len(outs) if many else spec,
        scratch_shapes=list(scratch),
        input_output_aliases=aliases or {},
        compiler_params=pltpu.CompilerParams(vmem_limit_bytes=40 * 2**20),
        cost_estimate=pl.CostEstimate(flops=flops, bytes_accessed=moved, transcendentals=0),
    )(*operands)


def local(coeffs, requests, repl_slot, repl_sign, pair_integrals):
    rows, cols = coeffs.shape
    peers = lax.axis_size("alpha")
    chips = lax.axis_size("beta")
    wanted = requests[0]
    cap = wanted.shape[1]
    width = peers * cap
    pairs = repl_slot.shape[0]

    ask = call(
        ask_kernel,
        jax.ShapeDtypeStruct((peers, 3 * cap), jnp.int32),
        (pltpu.with_memory_space_constraint(wanted.T, pltpu.HBM),),
        6 * peers * peers * cap,
        16 * peers * cap,
        scratch=[VMEM((cap, peers), jnp.int32)],
        spaces=[pltpu.HBM],
    )
    asked = lax.all_to_all(ask, "alpha", split_axis=0, concat_axis=0, tiled=True)
    asked_rows, asked_site = asked[:, :cap], asked[:, cap:]

    lanes = 1024 if (rows * pairs) % 1024 == 0 else rows * pairs
    group = 256 // pairs
    slot_rows = repl_slot.T.reshape(-1, lanes)
    sign_rows = repl_sign.T.reshape(-1, lanes)
    kron = jnp.kron(jnp.eye(group, dtype=BF16), pair_integrals.T)
    square = jax.ShapeDtypeStruct((width, width), BF16)
    high, low = call(
        coupling_kernel,
        [square, square],
        (slot_rows, sign_rows, kron),
        2 * rows * pairs * width * (width + 256),
        4 * width * width,
        scratch=[VMEM((width, width), F32)],
    )

    found = call(
        gather_kernel,
        jax.ShapeDtypeStruct((width, cols), BF16),
        (asked_rows, coeffs),
        2 * width * rows * cols,
        2 * (width + rows) * cols,
        scratch=[VMEM((width, cols), BF16), pltpu.SemaphoreType.DMA((4,))],
        out_space=pl.ANY,
    )
    fetched = lax.all_to_all(
        found.reshape(peers, cap, cols), "alpha", split_axis=0, concat_axis=0, tiled=True
    ).reshape(width, cols)

    to_sites, to_owners = call(
        contributions_kernel,
        [jax.ShapeDtypeStruct((peers, 2 * cap, cols // 2), BF16), jax.ShapeDtypeStruct((width, cols), BF16)],
        (high, low, fetched),
        4 * width * width * cols,
        4 * width * width + 6 * width * cols,
    )

    def site_sums(to_sites):
        to_sites = lax.all_to_all(to_sites, "alpha", split_axis=0, concat_axis=0, tiled=True)
        return call(
            lambda *refs: site_kernel(cap, *refs),
            jax.ShapeDtypeStruct((cols, rows), BF16),
            (asked_site, to_sites.reshape(2 * width, cols // 2)),
            2 * cols * width * cols,
            2 * (width + rows) * cols,
        )

    def nothing(to_sites):
        return jnp.zeros((cols, rows), BF16)

    places = [], [], []
    for j in range(chips):
        for h in range(2):
            for z in range(chips):
                l = (j - z - h * (chips // 2)) % chips
                part = 1 if 2 * z >= chips else 0 if 2 * l >= chips else 2
                places[part].append(((2 * j + h) * chips + z, (2 * z + h) * chips + l))
    axes = ("alpha", "beta")
    is_first = lax.axis_index("beta") < chips // 2
    first = lax.cond(is_first, site_sums, nothing, to_sites)
    first, to_sites = lax.optimization_barrier((first, to_sites))
    second = lax.cond(is_first, nothing, site_sums, to_sites)
    to_owners, second = lax.optimization_barrier((to_owners, second))
    third = lax.ppermute(first, axes, places[2])
    first = lax.ppermute(first, axes, places[0])
    second = lax.ppermute(second, axes, places[1])
    to_owners = call(copy_kernel, jax.ShapeDtypeStruct((width, cols), BF16), (to_owners,), 0, 4 * width * cols)
    to_owners = lax.all_to_all(
        to_owners.reshape(peers, cap, cols), "alpha", split_axis=0, concat_axis=0, tiled=True
    )
    block = jax.ShapeDtypeStruct((rows, cols), F32)
    first = call(turn_kernel, block, (first,), 15 * 10**8, 6 * rows * cols)
    turned = call(choose_kernel, block, (first, second), 32 * 10**8, 10 * rows * cols)
    part = call(
        own_kernel,
        block,
        (asked_rows, to_owners.reshape(width, cols), turned),
        3 * 10**10,
        10 * rows * cols,
    )
    return call(
        sigma_kernel,
        block,
        (part, third),
        rows * cols,
        10 * rows * cols,
        scratch=[VMEM((rows, cols), F32)],
        spaces=[pl.ANY],
        aliases={0: 0},
        out_space=pl.ANY,
    )


def solution(mesh):
    in_specs = (P("alpha", "beta"), P("alpha", None, None), P(None, "alpha"), P(None, "alpha"), P())
    out_specs = P("alpha", "beta")
    return jax.shard_map(local, mesh=mesh, in_specs=in_specs, out_specs=out_specs, check_vma=False)
```

```python
import jax
import jax.numpy as jnp
from jax import lax
from jax.experimental import pallas as pl
from jax.experimental.pallas import tpu as pltpu
from jax.sharding import PartitionSpec as P

F32 = jnp.float32
BF16 = jnp.bfloat16
VMEM = pltpu.VMEM


def flat_row(table, columns):
    n, m = table.shape
    width = n * m
    lane = lax.broadcasted_iota(jnp.int32, (m, width), 1)
    pick = (lane % m == lax.broadcasted_iota(jnp.int32, (m, width), 0)).astype(BF16)
    wide = jnp.dot(table.astype(F32).astype(BF16), pick, preferred_element_type=F32)
    lane = lax.broadcasted_iota(jnp.int32, (n, width), 1)
    mine = lane // m == lax.broadcasted_iota(jnp.int32, (n, width), 0)
    return jnp.sum(jnp.where(mine, wide, 0.0), axis=0, keepdims=True)


def one_hot(row, count):
    width = row.shape[1]
    middle = count // 2
    row = jnp.broadcast_to(row - middle, (16, width)).astype(BF16)
    line = lax.broadcasted_iota(jnp.int32, (16, width), 0).astype(F32).astype(BF16)
    one, zero = jnp.ones((16, width), BF16), jnp.zeros((16, width), BF16)
    lines = [jnp.where(row == line + jnp.asarray(n - middle, BF16), one, zero) for n in range(0, count, 16)]
    return jnp.concatenate(lines, axis=0)


def early_planes(chips):
    return 3 * chips // 8


def ask_kernel(from_ref, ask_ref, wanted_ref):
    pltpu.sync_copy(from_ref, wanted_ref)
    cap, peers = wanted_ref.shape
    chips = peers // 2
    plane = lax.axis_index("beta")
    site = lax.broadcasted_iota(jnp.int32, (peers, peers), 0)
    tile = lax.broadcasted_iota(jnp.int32, (peers, peers), 1)
    chip = site // 2 - plane - (site % 2) * (chips // 2 - 1)
    chip = jnp.where(chip < 0, chip + chips, chip)
    chip = jnp.where(chip < 0, chip + chips, chip)
    wanted = wanted_ref[...].astype(F32).astype(BF16)
    for part, source in enumerate((site, 2 * chip, 2 * chip + 1)):
        pick = (tile == source).astype(F32).astype(BF16)
        lists = lax.dot_general(pick, wanted, (((1,), (1,)), ((), ())), preferred_element_type=F32)
        ask_ref[:, part * cap : (part + 1) * cap] = lists.astype(jnp.int32)


def coupling_kernel(slot_ref, sign_ref, kron_ref, high_ref, low_ref, total_ref):
    chunks, lanes = slot_ref.shape
    width = total_ref.shape[0]
    side = kron_ref.shape[0]
    line = lax.broadcasted_iota(jnp.int32, (16, lanes), 0).astype(F32).astype(BF16)
    total_ref[...] = jnp.zeros_like(total_ref)

    def step(c, carry):
        slots = (slot_ref[pl.ds(c, 1), :] - width // 2).astype(F32)
        signs = sign_ref[pl.ds(c, 1), :].astype(F32)
        slots = jnp.broadcast_to(slots, (16, lanes)).astype(BF16)
        signs = jnp.broadcast_to(signs, (16, lanes)).astype(BF16)
        zero = jnp.zeros((16, lanes), BF16)
        rows = []
        for k in range(width // 16):
            base = jnp.asarray(16 * k - width // 2, BF16)
            rows.append(jnp.where(slots == line + base, signs, zero))
        table = jnp.concatenate(rows, axis=0)
        mixed = [
            jnp.dot(table[:, n : n + side], kron_ref[...], preferred_element_type=F32).astype(BF16)
            for n in range(0, lanes, side)
        ]
        mixed = jnp.concatenate(mixed, axis=1)
        total_ref[...] += lax.dot_general(
            table, mixed, (((1,), (1,)), ((), ())), preferred_element_type=F32
        )
        return carry

    lax.fori_loop(0, chunks, step, 0, unroll=True)
    high = total_ref[...].astype(BF16)
    high_ref[...] = high
    low_ref[...] = (total_ref[...] - high.astype(F32)).astype(BF16)


def gather_kernel(asked_ref, coeffs_ref, found_ref, held_ref, sems):
    rows = coeffs_ref.shape[0]
    peers, cap = asked_ref.shape
    pieces = sems.shape[0]
    line = lax.broadcasted_iota(jnp.int32, (cap, cap), 0)
    same = (line == lax.broadcasted_iota(jnp.int32, (cap, cap), 1)).astype(F32).astype(BF16)
    asked = asked_ref[...].astype(F32).astype(BF16)
    asked = lax.dot_general(same, asked, (((1,), (1,)), ((), ())), preferred_element_type=F32)
    lane = lax.broadcasted_iota(jnp.int32, (cap, rows), 1).astype(F32).astype(BF16)
    one, zero = jnp.ones((cap, rows), BF16), jnp.zeros((cap, rows), BF16)
    step = peers // pieces
    copies = []
    for n in range(pieces):
        tiles = range(n * step, (n + 1) * step)
        table = [
            jnp.where(jnp.broadcast_to(asked[:, t : t + 1], (cap, rows)).astype(BF16) == lane, one, zero)
            for t in tiles
        ]
        found = jnp.dot(jnp.concatenate(table, axis=0), coeffs_ref[...], preferred_element_type=F32)
        piece = pl.ds(n * step * cap, step * cap)
        held_ref[piece, :] = found.astype(BF16)
        copies.append(pltpu.make_async_copy(held_ref.at[piece, :], found_ref.at[piece, :], sems.at[n]))
        copies[n].start()
    for copy in copies:
        copy.wait()


def contributions_kernel(high_ref, low_ref, fetched_ref, sites_ref, owners_ref):
    sites, two_cap, half = sites_ref.shape
    chips = sites // 2
    plane = lax.axis_index("beta")
    fetched = fetched_ref[...]
    contrib = jnp.dot(high_ref[...], fetched, preferred_element_type=F32)
    contrib += jnp.dot(low_ref[...], fetched, preferred_element_type=F32)
    owners_ref[...] = contrib.astype(BF16)
    for j in range(chips):
        for h in range(2):
            chip = lax.rem(j + 2 * chips - plane - h * (chips // 2 - 1), chips)
            start = pl.multiple_of(chip * two_cap, two_cap)
            sites_ref[2 * j + h] = owners_ref[pl.ds(start, two_cap), h * half : (h + 1) * half]


def site_kernel(cap, asked_ref, contrib_ref, sent_ref):
    cols, rows = sent_ref.shape
    asked = flat_row(asked_ref[...], rows)
    lane = lax.broadcasted_iota(jnp.int32, asked.shape, 1)
    core = (lane // cap) % 2
    table = one_hot(asked + (core * rows).astype(F32), cols)
    sent_ref[...] = jnp.dot(table, contrib_ref[...], preferred_element_type=F32).astype(BF16)


def copy_kernel(from_ref, to_ref):
    to_ref[...] = from_ref[...]


def turn_kernel(sent_ref, asked_ref, turned_ref, table_ref):
    turned_ref[...] = sent_ref[...].astype(F32).T
    rows = turned_ref.shape[0]
    table_ref[...] = one_hot(flat_row(asked_ref[...], rows), rows)


def from_third(chips):
    source, place = lax.axis_index("alpha") // 2, lax.axis_index("beta")
    return jnp.logical_and(source < early_planes(chips), place < early_planes(chips))


def choose_kernel(first_ref, second_ref, turned_ref):
    chips = lax.axis_size("beta")
    from_first = lax.axis_index("alpha") // 2 < early_planes(chips)

    @pl.when(from_first)
    def _():
        turned_ref[...] = first_ref[...]

    @pl.when(jnp.logical_not(from_first))
    def _():
        turned_ref[...] = second_ref[...].astype(F32).T


def own_kernel(table_ref, contrib_ref, turned_ref, part_ref, sigma_ref, sem):
    part_ref[...] = jnp.dot(table_ref[...], contrib_ref[...], preferred_element_type=F32) + turned_ref[...]
    copy = pltpu.make_async_copy(part_ref, sigma_ref, sem)
    copy.start()
    copy.wait()


def sigma_kernel(before_ref, part_ref, third_ref, sigma_ref, held_ref):
    @pl.when(from_third(lax.axis_size("beta")))
    def _():
        held_ref[...] = part_ref[...] + third_ref[...].astype(F32).T
        pltpu.sync_copy(held_ref, sigma_ref)


def call(kernel, outs, operands, flops, moved, scratch=(), spaces=(), aliases=None, out_space=VMEM):
    many = isinstance(outs, (list, tuple))
    spec = pl.BlockSpec(memory_space=out_space)
    specs = [pl.BlockSpec(memory_space=space) for space in out_space] if isinstance(out_space, tuple) else None
    spaces = tuple(spaces) + (VMEM,) * (len(operands) - len(spaces))
    return pl.pallas_call(
        kernel,
        out_shape=outs,
        in_specs=[pl.BlockSpec(memory_space=space) for space in spaces],
        out_specs=specs or ([spec] * len(outs) if many else spec),
        scratch_shapes=list(scratch),
        input_output_aliases=aliases or {},
        compiler_params=pltpu.CompilerParams(vmem_limit_bytes=40 * 2**20),
        cost_estimate=pl.CostEstimate(flops=flops, bytes_accessed=moved, transcendentals=0),
    )(*operands)


def local(coeffs, requests, repl_slot, repl_sign, pair_integrals):
    rows, cols = coeffs.shape
    peers = lax.axis_size("alpha")
    chips = lax.axis_size("beta")
    wanted = requests[0]
    cap = wanted.shape[1]
    width = peers * cap
    pairs = repl_slot.shape[0]

    ask = call(
        ask_kernel,
        jax.ShapeDtypeStruct((peers, 3 * cap), jnp.int32),
        (pltpu.with_memory_space_constraint(wanted.T, pltpu.HBM),),
        6 * peers * peers * cap,
        16 * peers * cap,
        scratch=[VMEM((cap, peers), jnp.int32)],
        spaces=[pltpu.HBM],
    )
    asked = lax.all_to_all(ask, "alpha", split_axis=0, concat_axis=0, tiled=True)
    asked_rows, asked_site = asked[:, :cap], asked[:, cap:]

    lanes = 1024 if (rows * pairs) % 1024 == 0 else rows * pairs
    group = 256 // pairs
    slot_rows = repl_slot.T.reshape(-1, lanes)
    sign_rows = repl_sign.T.reshape(-1, lanes)
    kron = jnp.kron(jnp.eye(group, dtype=BF16), pair_integrals.T)
    square = jax.ShapeDtypeStruct((width, width), BF16)
    high, low = call(
        coupling_kernel,
        [square, square],
        (slot_rows, sign_rows, kron),
        2 * rows * pairs * width * (width + 256),
        4 * width * width,
        scratch=[VMEM((width, width), F32)],
    )

    found = call(
        gather_kernel,
        jax.ShapeDtypeStruct((width, cols), BF16),
        (asked_rows, coeffs),
        2 * width * rows * cols,
        2 * (width + rows) * cols,
        scratch=[VMEM((width, cols), BF16), pltpu.SemaphoreType.DMA((4,))],
        out_space=pl.ANY,
    )
    fetched = lax.all_to_all(
        found.reshape(peers, cap, cols), "alpha", split_axis=0, concat_axis=0, tiled=True
    ).reshape(width, cols)

    to_sites, to_owners = call(
        contributions_kernel,
        [jax.ShapeDtypeStruct((peers, 2 * cap, cols // 2), BF16), jax.ShapeDtypeStruct((width, cols), BF16)],
        (high, low, fetched),
        4 * width * width * cols,
        4 * width * width + 6 * width * cols,
    )

    def site_sums(to_sites):
        to_sites = lax.all_to_all(to_sites, "alpha", split_axis=0, concat_axis=0, tiled=True)
        return call(
            lambda *refs: site_kernel(cap, *refs),
            jax.ShapeDtypeStruct((cols, rows), BF16),
            (asked_site, to_sites.reshape(2 * width, cols // 2)),
            2 * cols * width * cols,
            2 * (width + rows) * cols,
        )

    def nothing(to_sites):
        return jnp.zeros((cols, rows), BF16)

    places = [], [], []
    for j in range(chips):
        for h in range(2):
            for z in range(chips):
                l = (j - z - h * (chips // 2 - 1)) % chips
                part = 1 if z >= early_planes(chips) else 0 if l >= early_planes(chips) else 2
                places[part].append(((2 * j + h) * chips + z, (2 * z + h) * chips + l))
    axes = ("alpha", "beta")
    is_first = lax.axis_index("beta") < early_planes(chips)
    first = lax.cond(is_first, site_sums, nothing, to_sites)
    first, to_sites = lax.optimization_barrier((first, to_sites))
    second = lax.cond(is_first, nothing, site_sums, to_sites)
    to_owners, second = lax.optimization_barrier((to_owners, second))
    third = lax.ppermute(first, axes, places[2])
    first = lax.ppermute(first, axes, places[0])
    second = lax.ppermute(second, axes, places[1])
    to_owners = call(copy_kernel, jax.ShapeDtypeStruct((width, cols), BF16), (to_owners,), 0, 4 * width * cols)
    to_owners = lax.all_to_all(
        to_owners.reshape(peers, cap, cols), "alpha", split_axis=0, concat_axis=0, tiled=True
    )
    block = jax.ShapeDtypeStruct((rows, cols), F32)
    table = jax.ShapeDtypeStruct((rows, width), BF16)
    first, table = call(turn_kernel, [block, table], (first, asked_rows), 15 * 10**8, 6 * rows * cols)
    turned = call(choose_kernel, block, (first, second), 32 * 10**8, 10 * rows * cols)
    part, sigma = call(
        own_kernel,
        [block, block],
        (table, to_owners.reshape(width, cols), turned),
        3 * 10**10,
        10 * rows * cols,
        scratch=[pltpu.SemaphoreType.DMA(())],
        out_space=(VMEM, pl.ANY),
    )
    return call(
        sigma_kernel,
        block,
        (sigma, part, third),
        rows * cols,
        10 * rows * cols,
        scratch=[VMEM((rows, cols), F32)],
        spaces=[pl.ANY],
        aliases={0: 0},
        out_space=pl.ANY,
    )


def solution(mesh):
    in_specs = (P("alpha", "beta"), P("alpha", None, None), P(None, "alpha"), P(None, "alpha"), P())
    out_specs = P("alpha", "beta")
    return jax.shard_map(local, mesh=mesh, in_specs=in_specs, out_specs=out_specs, check_vma=False)
```

```python
import jax
import jax.numpy as jnp
from jax import lax
from jax.experimental import pallas as pl
from jax.experimental.pallas import tpu as pltpu
from jax.sharding import PartitionSpec as P

F32 = jnp.float32
BF16 = jnp.bfloat16
VMEM = pltpu.VMEM


def flat_row(table, columns):
    n, m = table.shape
    width = n * m
    lane = lax.broadcasted_iota(jnp.int32, (m, width), 1)
    pick = (lane % m == lax.broadcasted_iota(jnp.int32, (m, width), 0)).astype(BF16)
    wide = jnp.dot(table.astype(F32).astype(BF16), pick, preferred_element_type=F32)
    lane = lax.broadcasted_iota(jnp.int32, (n, width), 1)
    mine = lane // m == lax.broadcasted_iota(jnp.int32, (n, width), 0)
    return jnp.sum(jnp.where(mine, wide, 0.0), axis=0, keepdims=True)


def one_hot(row, count):
    width = row.shape[1]
    middle = count // 2
    row = jnp.broadcast_to(row - middle, (16, width)).astype(BF16)
    line = lax.broadcasted_iota(jnp.int32, (16, width), 0).astype(F32).astype(BF16)
    one, zero = jnp.ones((16, width), BF16), jnp.zeros((16, width), BF16)
    lines = [jnp.where(row == line + jnp.asarray(n - middle, BF16), one, zero) for n in range(0, count, 16)]
    return jnp.concatenate(lines, axis=0)


def early_planes(chips):
    return 3 * chips // 8


def ask_kernel(from_ref, ask_ref, wanted_ref):
    pltpu.sync_copy(from_ref, wanted_ref)
    cap, peers = wanted_ref.shape
    chips = peers // 2
    plane = lax.axis_index("beta")
    site = lax.broadcasted_iota(jnp.int32, (peers, peers), 0)
    tile = lax.broadcasted_iota(jnp.int32, (peers, peers), 1)
    chip = site // 2 - plane - (site % 2) * (chips // 2 - 1)
    chip = jnp.where(chip < 0, chip + chips, chip)
    chip = jnp.where(chip < 0, chip + chips, chip)
    wanted = wanted_ref[...].astype(F32).astype(BF16)
    for part, source in enumerate((site, 2 * chip, 2 * chip + 1)):
        pick = (tile == source).astype(F32).astype(BF16)
        lists = lax.dot_general(pick, wanted, (((1,), (1,)), ((), ())), preferred_element_type=F32)
        ask_ref[:, part * cap : (part + 1) * cap] = lists.astype(jnp.int32)


def coupling_kernel(slot_ref, sign_ref, kron_ref, high_ref, low_ref, total_ref):
    chunks, lanes = slot_ref.shape
    width = total_ref.shape[0]
    side = kron_ref.shape[0]
    line = lax.broadcasted_iota(jnp.int32, (16, lanes), 0).astype(F32).astype(BF16)
    total_ref[...] = jnp.zeros_like(total_ref)

    def step(c, carry):
        slots = (slot_ref[pl.ds(c, 1), :] - width // 2).astype(F32)
        signs = sign_ref[pl.ds(c, 1), :].astype(F32)
        slots = jnp.broadcast_to(slots, (16, lanes)).astype(BF16)
        signs = jnp.broadcast_to(signs, (16, lanes)).astype(BF16)
        zero = jnp.zeros((16, lanes), BF16)
        rows = []
        for k in range(width // 16):
            base = jnp.asarray(16 * k - width // 2, BF16)
            rows.append(jnp.where(slots == line + base, signs, zero))
        table = jnp.concatenate(rows, axis=0)
        mixed = [
            jnp.dot(table[:, n : n + side], kron_ref[...], preferred_element_type=F32).astype(BF16)
            for n in range(0, lanes, side)
        ]
        mixed = jnp.concatenate(mixed, axis=1)
        total_ref[...] += lax.dot_general(
            table, mixed, (((1,), (1,)), ((), ())), preferred_element_type=F32
        )
        return carry

    lax.fori_loop(0, chunks, step, 0, unroll=True)
    high = total_ref[...].astype(BF16)
    high_ref[...] = high
    low_ref[...] = (total_ref[...] - high.astype(F32)).astype(BF16)


def gather_kernel(asked_ref, coeffs_ref, found_ref, held_ref, sems):
    rows = coeffs_ref.shape[0]
    peers, cap = asked_ref.shape
    pieces = sems.shape[0]
    line = lax.broadcasted_iota(jnp.int32, (cap, cap), 0)
    same = (line == lax.broadcasted_iota(jnp.int32, (cap, cap), 1)).astype(F32).astype(BF16)
    asked = asked_ref[...].astype(F32).astype(BF16)
    asked = lax.dot_general(same, asked, (((1,), (1,)), ((), ())), preferred_element_type=F32)
    lane = lax.broadcasted_iota(jnp.int32, (cap, rows), 1).astype(F32).astype(BF16)
    one, zero = jnp.ones((cap, rows), BF16), jnp.zeros((cap, rows), BF16)
    step = peers // pieces
    copies = []
    for n in range(pieces):
        tiles = range(n * step, (n + 1) * step)
        table = [
            jnp.where(jnp.broadcast_to(asked[:, t : t + 1], (cap, rows)).astype(BF16) == lane, one, zero)
            for t in tiles
        ]
        found = jnp.dot(jnp.concatenate(table, axis=0), coeffs_ref[...], preferred_element_type=F32)
        piece = pl.ds(n * step * cap, step * cap)
        held_ref[piece, :] = found.astype(BF16)
        copies.append(pltpu.make_async_copy(held_ref.at[piece, :], found_ref.at[piece, :], sems.at[n]))
        copies[n].start()
    for copy in copies:
        copy.wait()


def contributions_kernel(high_ref, low_ref, fetched_ref, sites_ref, owners_ref):
    sites, two_cap, half = sites_ref.shape
    chips = sites // 2
    plane = lax.axis_index("beta")
    fetched = fetched_ref[...]
    contrib = jnp.dot(high_ref[...], fetched, preferred_element_type=F32)
    contrib += jnp.dot(low_ref[...], fetched, preferred_element_type=F32)
    owners_ref[...] = contrib.astype(BF16)
    for j in range(chips):
        for h in range(2):
            chip = lax.rem(j + 2 * chips - plane - h * (chips // 2 - 1), chips)
            start = pl.multiple_of(chip * two_cap, two_cap)
            sites_ref[2 * j + h] = owners_ref[pl.ds(start, two_cap), h * half : (h + 1) * half]


def site_kernel(cap, asked_ref, contrib_ref, sent_ref):
    cols, rows = sent_ref.shape
    asked = flat_row(asked_ref[...], rows)
    lane = lax.broadcasted_iota(jnp.int32, asked.shape, 1)
    core = (lane // cap) % 2
    table = one_hot(asked + (core * rows).astype(F32), cols)
    sent_ref[...] = jnp.dot(table, contrib_ref[...], preferred_element_type=F32).astype(BF16)


def copy_kernel(from_ref, to_ref):
    to_ref[...] = from_ref[...]


def turn_kernel(sent_ref, asked_ref, turned_ref, table_ref):
    turned_ref[...] = sent_ref[...].astype(F32).T
    rows = turned_ref.shape[0]
    table_ref[...] = one_hot(flat_row(asked_ref[...], rows), rows)


def from_third(chips):
    source, place = lax.axis_index("alpha") // 2, lax.axis_index("beta")
    return jnp.logical_and(source < early_planes(chips), place < early_planes(chips))


def choose_kernel(first_ref, second_ref, turned_ref):
    chips = lax.axis_size("beta")
    from_first = lax.axis_index("alpha") // 2 < early_planes(chips)

    @pl.when(from_first)
    def _():
        turned_ref[...] = first_ref[...]

    @pl.when(jnp.logical_not(from_first))
    def _():
        turned_ref[...] = second_ref[...].astype(F32).T


def own_kernel(table_ref, contrib_ref, turned_ref, part_ref, sigma_ref, sems):
    rows = part_ref.shape[0]
    step = rows // 2
    copies = []
    for n in range(2):
        piece = pl.ds(n * step, step)
        own = jnp.dot(table_ref[piece, :], contrib_ref[...], preferred_element_type=F32)
        part_ref[piece, :] = own + turned_ref[piece, :]
        copies.append(pltpu.make_async_copy(part_ref.at[piece, :], sigma_ref.at[piece, :], sems.at[n]))
        copies[n].start()
    for copy in copies:
        copy.wait()


def sigma_kernel(before_ref, part_ref, third_ref, sigma_ref, held_ref):
    @pl.when(from_third(lax.axis_size("beta")))
    def _():
        held_ref[...] = part_ref[...] + third_ref[...].astype(F32).T
        pltpu.sync_copy(held_ref, sigma_ref)


def call(kernel, outs, operands, flops, moved, scratch=(), spaces=(), aliases=None, out_space=VMEM):
    many = isinstance(outs, (list, tuple))
    spec = pl.BlockSpec(memory_space=out_space)
    specs = [pl.BlockSpec(memory_space=space) for space in out_space] if isinstance(out_space, tuple) else None
    spaces = tuple(spaces) + (VMEM,) * (len(operands) - len(spaces))
    return pl.pallas_call(
        kernel,
        out_shape=outs,
        in_specs=[pl.BlockSpec(memory_space=space) for space in spaces],
        out_specs=specs or ([spec] * len(outs) if many else spec),
        scratch_shapes=list(scratch),
        input_output_aliases=aliases or {},
        compiler_params=pltpu.CompilerParams(vmem_limit_bytes=40 * 2**20),
        cost_estimate=pl.CostEstimate(flops=flops, bytes_accessed=moved, transcendentals=0),
    )(*operands)


def local(coeffs, requests, repl_slot, repl_sign, pair_integrals):
    rows, cols = coeffs.shape
    peers = lax.axis_size("alpha")
    chips = lax.axis_size("beta")
    wanted = requests[0]
    cap = wanted.shape[1]
    width = peers * cap
    pairs = repl_slot.shape[0]

    ask = call(
        ask_kernel,
        jax.ShapeDtypeStruct((peers, 3 * cap), jnp.int32),
        (pltpu.with_memory_space_constraint(wanted.T, pltpu.HBM),),
        6 * peers * peers * cap,
        16 * peers * cap,
        scratch=[VMEM((cap, peers), jnp.int32)],
        spaces=[pltpu.HBM],
    )
    asked = lax.all_to_all(ask, "alpha", split_axis=0, concat_axis=0, tiled=True)
    asked_rows, asked_site = asked[:, :cap], asked[:, cap:]

    lanes = 1024 if (rows * pairs) % 1024 == 0 else rows * pairs
    group = 256 // pairs
    slot_rows = repl_slot.T.reshape(-1, lanes)
    sign_rows = repl_sign.T.reshape(-1, lanes)
    kron = jnp.kron(jnp.eye(group, dtype=BF16), pair_integrals.T)
    square = jax.ShapeDtypeStruct((width, width), BF16)
    high, low = call(
        coupling_kernel,
        [square, square],
        (slot_rows, sign_rows, kron),
        2 * rows * pairs * width * (width + 256),
        4 * width * width,
        scratch=[VMEM((width, width), F32)],
    )

    found = call(
        gather_kernel,
        jax.ShapeDtypeStruct((width, cols), BF16),
        (asked_rows, coeffs),
        2 * width * rows * cols,
        2 * (width + rows) * cols,
        scratch=[VMEM((width, cols), BF16), pltpu.SemaphoreType.DMA((4,))],
        out_space=pl.ANY,
    )
    fetched = lax.all_to_all(
        found.reshape(peers, cap, cols), "alpha", split_axis=0, concat_axis=0, tiled=True
    ).reshape(width, cols)

    to_sites, to_owners = call(
        contributions_kernel,
        [jax.ShapeDtypeStruct((peers, 2 * cap, cols // 2), BF16), jax.ShapeDtypeStruct((width, cols), BF16)],
        (high, low, fetched),
        4 * width * width * cols,
        4 * width * width + 6 * width * cols,
    )

    def site_sums(to_sites):
        to_sites = lax.all_to_all(to_sites, "alpha", split_axis=0, concat_axis=0, tiled=True)
        return call(
            lambda *refs: site_kernel(cap, *refs),
            jax.ShapeDtypeStruct((cols, rows), BF16),
            (asked_site, to_sites.reshape(2 * width, cols // 2)),
            2 * cols * width * cols,
            2 * (width + rows) * cols,
        )

    def nothing(to_sites):
        return jnp.zeros((cols, rows), BF16)

    places = [], [], []
    for j in range(chips):
        for h in range(2):
            for z in range(chips):
                l = (j - z - h * (chips // 2 - 1)) % chips
                part = 1 if z >= early_planes(chips) else 0 if l >= early_planes(chips) else 2
                places[part].append(((2 * j + h) * chips + z, (2 * z + h) * chips + l))
    axes = ("alpha", "beta")
    is_first = lax.axis_index("beta") < early_planes(chips)
    first = lax.cond(is_first, site_sums, nothing, to_sites)
    first, to_sites = lax.optimization_barrier((first, to_sites))
    second = lax.cond(is_first, nothing, site_sums, to_sites)
    to_owners, second = lax.optimization_barrier((to_owners, second))
    third = lax.ppermute(first, axes, places[2])
    first = lax.ppermute(first, axes, places[0])
    second = lax.ppermute(second, axes, places[1])
    to_owners = call(copy_kernel, jax.ShapeDtypeStruct((width, cols), BF16), (to_owners,), 0, 4 * width * cols)
    to_owners = lax.all_to_all(
        to_owners.reshape(peers, cap, cols), "alpha", split_axis=0, concat_axis=0, tiled=True
    )
    block = jax.ShapeDtypeStruct((rows, cols), F32)
    table = jax.ShapeDtypeStruct((rows, width), BF16)
    first, table = call(turn_kernel, [block, table], (first, asked_rows), 15 * 10**8, 6 * rows * cols)
    turned = call(choose_kernel, block, (first, second), 32 * 10**8, 10 * rows * cols)
    part, sigma = call(
        own_kernel,
        [block, block],
        (table, to_owners.reshape(width, cols), turned),
        3 * 10**10,
        10 * rows * cols,
        scratch=[pltpu.SemaphoreType.DMA((2,))],
        out_space=(VMEM, pl.ANY),
    )
    return call(
        sigma_kernel,
        block,
        (sigma, part, third),
        rows * cols,
        10 * rows * cols,
        scratch=[VMEM((rows, cols), F32)],
        spaces=[pl.ANY],
        aliases={0: 0},
        out_space=pl.ANY,
    )


def solution(mesh):
    in_specs = (P("alpha", "beta"), P("alpha", None, None), P(None, "alpha"), P(None, "alpha"), P())
    out_specs = P("alpha", "beta")
    return jax.shard_map(local, mesh=mesh, in_specs=in_specs, out_specs=out_specs, check_vma=False)
```

```python
import jax
import jax.numpy as jnp
from jax import lax
from jax.experimental import pallas as pl
from jax.experimental.pallas import tpu as pltpu
from jax.sharding import PartitionSpec as P

F32 = jnp.float32
BF16 = jnp.bfloat16
VMEM = pltpu.VMEM


def flat_row(table, columns):
    n, m = table.shape
    width = n * m
    lane = lax.broadcasted_iota(jnp.int32, (m, width), 1)
    pick = (lane % m == lax.broadcasted_iota(jnp.int32, (m, width), 0)).astype(BF16)
    wide = jnp.dot(table.astype(F32).astype(BF16), pick, preferred_element_type=F32)
    lane = lax.broadcasted_iota(jnp.int32, (n, width), 1)
    mine = lane // m == lax.broadcasted_iota(jnp.int32, (n, width), 0)
    return jnp.sum(jnp.where(mine, wide, 0.0), axis=0, keepdims=True)


def one_hot(row, count):
    width = row.shape[1]
    middle = count // 2
    row = jnp.broadcast_to(row - middle, (16, width)).astype(BF16)
    line = lax.broadcasted_iota(jnp.int32, (16, width), 0).astype(F32).astype(BF16)
    one, zero = jnp.ones((16, width), BF16), jnp.zeros((16, width), BF16)
    lines = [jnp.where(row == line + jnp.asarray(n - middle, BF16), one, zero) for n in range(0, count, 16)]
    return jnp.concatenate(lines, axis=0)


def early_planes(chips):
    return 3 * chips // 8


def ask_kernel(from_ref, ask_ref, wanted_ref, sem):
    copy = pltpu.make_async_copy(from_ref, wanted_ref, sem)
    copy.start()
    cap, peers = wanted_ref.shape
    chips = peers // 2
    plane = lax.axis_index("beta")
    site = lax.broadcasted_iota(jnp.int32, (peers, peers), 0)
    tile = lax.broadcasted_iota(jnp.int32, (peers, peers), 1)
    chip = site // 2 - plane - (site % 2) * (chips // 2 - 1)
    chip = jnp.where(chip < 0, chip + chips, chip)
    chip = jnp.where(chip < 0, chip + chips, chip)
    picks = [(tile == source).astype(F32).astype(BF16) for source in (site, 2 * chip, 2 * chip + 1)]
    copy.wait()
    wanted = wanted_ref[...].astype(F32).astype(BF16)
    for part, pick in enumerate(picks):
        lists = lax.dot_general(pick, wanted, (((1,), (1,)), ((), ())), preferred_element_type=F32)
        ask_ref[:, part * cap : (part + 1) * cap] = lists.astype(jnp.int32)


def coupling_kernel(slot_ref, sign_ref, kron_ref, high_ref, low_ref, total_ref):
    chunks, lanes = slot_ref.shape
    width = total_ref.shape[0]
    side = kron_ref.shape[0]
    line = lax.broadcasted_iota(jnp.int32, (16, lanes), 0).astype(F32).astype(BF16)
    total_ref[...] = jnp.zeros_like(total_ref)

    def step(c, carry):
        slots = (slot_ref[pl.ds(c, 1), :] - width // 2).astype(F32)
        signs = sign_ref[pl.ds(c, 1), :].astype(F32)
        slots = jnp.broadcast_to(slots, (16, lanes)).astype(BF16)
        signs = jnp.broadcast_to(signs, (16, lanes)).astype(BF16)
        zero = jnp.zeros((16, lanes), BF16)
        rows = []
        for k in range(width // 16):
            base = jnp.asarray(16 * k - width // 2, BF16)
            rows.append(jnp.where(slots == line + base, signs, zero))
        table = jnp.concatenate(rows, axis=0)
        mixed = [
            jnp.dot(table[:, n : n + side], kron_ref[...], preferred_element_type=F32).astype(BF16)
            for n in range(0, lanes, side)
        ]
        mixed = jnp.concatenate(mixed, axis=1)
        total_ref[...] += lax.dot_general(
            table, mixed, (((1,), (1,)), ((), ())), preferred_element_type=F32
        )
        return carry

    lax.fori_loop(0, chunks, step, 0, unroll=True)
    high = total_ref[...].astype(BF16)
    high_ref[...] = high
    low_ref[...] = (total_ref[...] - high.astype(F32)).astype(BF16)


def gather_kernel(asked_ref, coeffs_ref, found_ref, held_ref, sems):
    rows = coeffs_ref.shape[0]
    peers, cap = asked_ref.shape
    pieces = sems.shape[0]
    line = lax.broadcasted_iota(jnp.int32, (cap, cap), 0)
    same = (line == lax.broadcasted_iota(jnp.int32, (cap, cap), 1)).astype(F32).astype(BF16)
    asked = asked_ref[...].astype(F32).astype(BF16)
    asked = lax.dot_general(same, asked, (((1,), (1,)), ((), ())), preferred_element_type=F32)
    lane = lax.broadcasted_iota(jnp.int32, (cap, rows), 1).astype(F32).astype(BF16)
    one, zero = jnp.ones((cap, rows), BF16), jnp.zeros((cap, rows), BF16)
    step = peers // pieces
    copies = []
    for n in range(pieces):
        tiles = range(n * step, (n + 1) * step)
        table = [
            jnp.where(jnp.broadcast_to(asked[:, t : t + 1], (cap, rows)).astype(BF16) == lane, one, zero)
            for t in tiles
        ]
        found = jnp.dot(jnp.concatenate(table, axis=0), coeffs_ref[...], preferred_element_type=F32)
        piece = pl.ds(n * step * cap, step * cap)
        held_ref[piece, :] = found.astype(BF16)
        copies.append(pltpu.make_async_copy(held_ref.at[piece, :], found_ref.at[piece, :], sems.at[n]))
        copies[n].start()
    for copy in copies:
        copy.wait()


def contributions_kernel(high_ref, low_ref, fetched_ref, sites_ref, owners_ref):
    sites, two_cap, half = sites_ref.shape
    chips = sites // 2
    plane = lax.axis_index("beta")
    fetched = fetched_ref[...]
    contrib = jnp.dot(high_ref[...], fetched, preferred_element_type=F32)
    contrib += jnp.dot(low_ref[...], fetched, preferred_element_type=F32)
    owners_ref[...] = contrib.astype(BF16)
    for j in range(chips):
        for h in range(2):
            chip = lax.rem(j + 2 * chips - plane - h * (chips // 2 - 1), chips)
            start = pl.multiple_of(chip * two_cap, two_cap)
            sites_ref[2 * j + h] = owners_ref[pl.ds(start, two_cap), h * half : (h + 1) * half]


def site_kernel(cap, asked_ref, contrib_ref, sent_ref):
    cols, rows = sent_ref.shape
    asked = flat_row(asked_ref[...], rows)
    lane = lax.broadcasted_iota(jnp.int32, asked.shape, 1)
    core = (lane // cap) % 2
    table = one_hot(asked + (core * rows).astype(F32), cols)
    sent_ref[...] = jnp.dot(table, contrib_ref[...], preferred_element_type=F32).astype(BF16)


def copy_kernel(from_ref, to_ref):
    to_ref[...] = from_ref[...]


def turn_kernel(sent_ref, asked_ref, turned_ref, table_ref):
    turned_ref[...] = sent_ref[...].astype(F32).T
    rows = turned_ref.shape[0]
    table_ref[...] = one_hot(flat_row(asked_ref[...], rows), rows)


def from_third(chips):
    source, place = lax.axis_index("alpha") // 2, lax.axis_index("beta")
    return jnp.logical_and(source < early_planes(chips), place < early_planes(chips))


def choose_kernel(first_ref, second_ref, turned_ref):
    chips = lax.axis_size("beta")
    from_first = lax.axis_index("alpha") // 2 < early_planes(chips)

    @pl.when(from_first)
    def _():
        turned_ref[...] = first_ref[...]

    @pl.when(jnp.logical_not(from_first))
    def _():
        turned_ref[...] = second_ref[...].astype(F32).T


def own_kernel(table_ref, contrib_ref, turned_ref, part_ref, sigma_ref, sems):
    rows = part_ref.shape[0]
    step = rows // 2
    copies = []
    for n in range(2):
        piece = pl.ds(n * step, step)
        own = jnp.dot(table_ref[piece, :], contrib_ref[...], preferred_element_type=F32)
        part_ref[piece, :] = own + turned_ref[piece, :]
        copies.append(pltpu.make_async_copy(part_ref.at[piece, :], sigma_ref.at[piece, :], sems.at[n]))
        copies[n].start()
    for copy in copies:
        copy.wait()


def sigma_kernel(before_ref, part_ref, third_ref, sigma_ref, held_ref):
    @pl.when(from_third(lax.axis_size("beta")))
    def _():
        held_ref[...] = part_ref[...] + third_ref[...].astype(F32).T
        pltpu.sync_copy(held_ref, sigma_ref)


def call(kernel, outs, operands, flops, moved, scratch=(), spaces=(), aliases=None, out_space=VMEM):
    many = isinstance(outs, (list, tuple))
    spec = pl.BlockSpec(memory_space=out_space)
    specs = [pl.BlockSpec(memory_space=space) for space in out_space] if isinstance(out_space, tuple) else None
    spaces = tuple(spaces) + (VMEM,) * (len(operands) - len(spaces))
    return pl.pallas_call(
        kernel,
        out_shape=outs,
        in_specs=[pl.BlockSpec(memory_space=space) for space in spaces],
        out_specs=specs or ([spec] * len(outs) if many else spec),
        scratch_shapes=list(scratch),
        input_output_aliases=aliases or {},
        compiler_params=pltpu.CompilerParams(vmem_limit_bytes=40 * 2**20),
        cost_estimate=pl.CostEstimate(flops=flops, bytes_accessed=moved, transcendentals=0),
    )(*operands)


def local(coeffs, requests, repl_slot, repl_sign, pair_integrals):
    rows, cols = coeffs.shape
    peers = lax.axis_size("alpha")
    chips = lax.axis_size("beta")
    wanted = requests[0]
    cap = wanted.shape[1]
    width = peers * cap
    pairs = repl_slot.shape[0]

    ask = call(
        ask_kernel,
        jax.ShapeDtypeStruct((peers, 3 * cap), jnp.int32),
        (pltpu.with_memory_space_constraint(wanted.T, pltpu.HBM),),
        6 * peers * peers * cap,
        16 * peers * cap,
        scratch=[VMEM((cap, peers), jnp.int32), pltpu.SemaphoreType.DMA(())],
        spaces=[pltpu.HBM],
    )
    asked = lax.all_to_all(ask, "alpha", split_axis=0, concat_axis=0, tiled=True)
    asked_rows, asked_site = asked[:, :cap], asked[:, cap:]

    lanes = 1024 if (rows * pairs) % 1024 == 0 else rows * pairs
    group = 256 // pairs
    slot_rows = repl_slot.T.reshape(-1, lanes)
    sign_rows = repl_sign.T.reshape(-1, lanes)
    kron = jnp.kron(jnp.eye(group, dtype=BF16), pair_integrals.T)
    square = jax.ShapeDtypeStruct((width, width), BF16)
    high, low = call(
        coupling_kernel,
        [square, square],
        (slot_rows, sign_rows, kron),
        2 * rows * pairs * width * (width + 256),
        4 * width * width,
        scratch=[VMEM((width, width), F32)],
    )

    found = call(
        gather_kernel,
        jax.ShapeDtypeStruct((width, cols), BF16),
        (asked_rows, coeffs),
        2 * width * rows * cols,
        2 * (width + rows) * cols,
        scratch=[VMEM((width, cols), BF16), pltpu.SemaphoreType.DMA((4,))],
        out_space=pl.ANY,
    )
    fetched = lax.all_to_all(
        found.reshape(peers, cap, cols), "alpha", split_axis=0, concat_axis=0, tiled=True
    ).reshape(width, cols)

    to_sites, to_owners = call(
        contributions_kernel,
        [jax.ShapeDtypeStruct((peers, 2 * cap, cols // 2), BF16), jax.ShapeDtypeStruct((width, cols), BF16)],
        (high, low, fetched),
        4 * width * width * cols,
        4 * width * width + 6 * width * cols,
    )

    def site_sums(to_sites):
        to_sites = lax.all_to_all(to_sites, "alpha", split_axis=0, concat_axis=0, tiled=True)
        return call(
            lambda *refs: site_kernel(cap, *refs),
            jax.ShapeDtypeStruct((cols, rows), BF16),
            (asked_site, to_sites.reshape(2 * width, cols // 2)),
            2 * cols * width * cols,
            2 * (width + rows) * cols,
        )

    def nothing(to_sites):
        return jnp.zeros((cols, rows), BF16)

    places = [], [], []
    for j in range(chips):
        for h in range(2):
            for z in range(chips):
                l = (j - z - h * (chips // 2 - 1)) % chips
                part = 1 if z >= early_planes(chips) else 0 if l >= early_planes(chips) else 2
                places[part].append(((2 * j + h) * chips + z, (2 * z + h) * chips + l))
    axes = ("alpha", "beta")
    is_first = lax.axis_index("beta") < early_planes(chips)
    first = lax.cond(is_first, site_sums, nothing, to_sites)
    first, to_sites = lax.optimization_barrier((first, to_sites))
    second = lax.cond(is_first, nothing, site_sums, to_sites)
    to_owners, second = lax.optimization_barrier((to_owners, second))
    third = lax.ppermute(first, axes, places[2])
    first = lax.ppermute(first, axes, places[0])
    second = lax.ppermute(second, axes, places[1])
    to_owners = call(copy_kernel, jax.ShapeDtypeStruct((width, cols), BF16), (to_owners,), 0, 4 * width * cols)
    to_owners = lax.all_to_all(
        to_owners.reshape(peers, cap, cols), "alpha", split_axis=0, concat_axis=0, tiled=True
    )
    block = jax.ShapeDtypeStruct((rows, cols), F32)
    table = jax.ShapeDtypeStruct((rows, width), BF16)
    first, table = call(turn_kernel, [block, table], (first, asked_rows), 15 * 10**8, 6 * rows * cols)
    turned = call(choose_kernel, block, (first, second), 32 * 10**8, 10 * rows * cols)
    part, sigma = call(
        own_kernel,
        [block, block],
        (table, to_owners.reshape(width, cols), turned),
        3 * 10**10,
        10 * rows * cols,
        scratch=[pltpu.SemaphoreType.DMA((2,))],
        out_space=(VMEM, pl.ANY),
    )
    return call(
        sigma_kernel,
        block,
        (sigma, part, third),
        rows * cols,
        10 * rows * cols,
        scratch=[VMEM((rows, cols), F32)],
        spaces=[pl.ANY],
        aliases={0: 0},
        out_space=pl.ANY,
    )


def solution(mesh):
    in_specs = (P("alpha", "beta"), P("alpha", None, None), P(None, "alpha"), P(None, "alpha"), P())
    out_specs = P("alpha", "beta")
    return jax.shard_map(local, mesh=mesh, in_specs=in_specs, out_specs=out_specs, check_vma=False)
```
